32 devices in a mesh: dom: 2 (over y), dp: 2 (over x), expert: 8 (over z, core).
Axes of the slice: x: 2, y: 2, z: 4, core: 2. Of those that a mesh axis runs over, the one named last changes fastest.
Arguments:
- hidden: bfloat16 [4, 8, 16, 66, 1280], P(('dom', 'dp'), None, 'expert'), parts along dimension 0, may hold values from -6 to 6
- expert_choice_index: int32 [4096, 8], P(('dom', 'dp', 'expert')), parts along dimension 0, may hold values from 0 to 15, all different within a row; in each aligned block of 128 rows (0 to 127, 128 to 255, ...) at most 66 rows name the same one
- gates: float32 [4096, 8], P(('dom', 'dp', 'expert')), parts along dimension 0, may hold values from 0.02 to 0.3
- down_adapter_hidden: bfloat16 [16, 32, 1280], P('expert', None, 'dp'), may hold values from -0.15625 to 0.15625
- hidden_tangent: bfloat16 [32, 32, 1280], P(('dom', 'expert'), None, 'dp'), parts along dimension 0, may hold values from -0.15625 to 0.15625
- down_adapter_output: bfloat16 [16, 32, 3584], P('expert'), may hold values from -1 to 1
- output_tangent_factor: bfloat16 [32, 32, 3584], P(('dom', 'expert')), parts along dimension 0, may hold values from -1 to 1
Outputs:
- grad_a: float32 [32, 32, 1280], P(('dom', 'expert'), None, 'dp'), parts along dimension 0
- grad_b: float32 [32, 32, 3584], P(('dom', 'expert'), None, 'dp'), parts along dimension 0
The draws below stay inside these ranges and needn't reach their ends.
There are 2 independent parts, one for each index of `dom`. The reference program is written for one: setup_inputs(seed, part) draws one part's arguments, and reference() takes and returns one part's arrays. A program takes and returns all parts, laid end to end along the dimension named above; an argument that names none is the same for every part. Nothing has to cross between parts.
Inputs may be any that keep to these rules, and one draw needn't show every extreme that they name: `expert_choice_index`: each row names 8 different experts. In each aligned block of 128 rows (the rows of one device) no expert is named by more than 66 rows, and in every draw some block names some expert exactly 66 times.
All inputs are finite; a program needn't handle non-finite values.
Results may differ from the reference program's by a relative error of at most 0.0035.
Values may be sent and summed in bfloat16 or wider, within the bound.
A program may use at most 128 MiB of HBM per device.

```python
import math
import jax
import jax.numpy as jnp
import numpy as np
from jax import lax

MODEL_WIDTH = 3584
HIDDEN_HALF = 1280
ADAPTER_RANK = 32
TOP = 8
TOK_DEV = 128
ROUTED_EXPERTS = 16
TOKENS = 2048
CAP = 66
N_DP = 2
N_EXPERT = 8


def shard_levels(rng, extent, pieces, least, largest):
    def one(dim, blocks):
        heights = jax.random.uniform(jax.random.fold_in(jax.random.fold_in(rng, 6), dim), (blocks,), jnp.float32, least / len(pieces), largest / len(pieces))
        return jnp.repeat(jnp.exp(heights), extent[dim] // blocks).reshape((-1,) + (1,) * (len(extent) - dim - 1))

    loudness = one(*pieces[0])
    for cut in pieces[1:]:
        loudness = loudness * one(*cut)
    return loudness


def deal_out(own_key, own, number, rows, number_of, top, reach, skew):
    sequence = jax.random.permutation(own_key, number_of)
    heavy_load, usual = load_shares(number_of, rows * top, reach, skew, True), load_shares(number_of, rows * top, reach, skew, False)
    places = jnp.arange(number_of)

    def named(lengths, turn):
        used = int((lengths > 0).sum())
        fixed = max(1, used // 4)
        passed = fixed + (places - fixed + turn * (used - fixed)) % max(1, number_of - fixed)
        return jnp.zeros((number_of,), jnp.int32).at[sequence[jnp.where(places < fixed, places, passed)]].set(jnp.asarray(lengths, jnp.int32))

    lengths = jnp.where(number % 4 == 0, named(heavy_load, number // 4), named(usual, number - number // 4 - 1))
    mixed = jax.random.permutation(jax.random.fold_in(own, 3), number_of)
    donor, receiver = mixed[0:number_of // 2 * 2:2], mixed[1:number_of // 2 * 2:2]
    room = jnp.minimum(lengths[donor] - 1, reach - lengths[receiver]) // 2
    room = jnp.where((donor == sequence[0]) | (receiver == sequence[0]) | (lengths[receiver] == 0), 0, jnp.maximum(room, 0))
    passed = jax.random.randint(jax.random.fold_in(own, 4), (number_of // 2,), 0, 1 << 20) % (room + 1)
    lengths = lengths.at[donor].add(-passed).at[receiver].add(passed)
    items = jnp.searchsorted(jnp.cumsum(lengths), jnp.arange(rows * top), side="right").astype(jnp.int32)
    grid = items.reshape(top, rows).T
    grid = grid[jax.random.permutation(jax.random.fold_in(own, 1), rows)]
    turn = jax.random.randint(jax.random.fold_in(own, 2), (rows, 1), 0, top)
    return jnp.take_along_axis(grid, (jnp.arange(top)[None, :] + turn) % top, axis=1)


def load_shares(amount, total, most, skew, full):
    portions = [(1 << 20) // math.isqrt(rank ** skew) + 1 for rank in range(1, amount + 1)]
    largest = most if full else min(most, max(-(-total // amount), total * portions[0] // sum(portions)))
    least = 1 if total - largest >= amount - 1 else 0
    given, surplus = [largest] + [least] * (amount - 1), total - largest - least * (amount - 1)
    while surplus > 0:
        movable = [i for i in range(1, amount) if given[i] < largest] or [i for i in range(1, amount) if given[i] < most]
        pool, remaining = sum([portions[i] for i in movable]), surplus
        for i in movable:
            more = min(most - given[i], max(1, remaining * portions[i] // pool), surplus)
            given[i] = given[i] + more
            surplus = surplus - more
    return np.array(given)


def noise(own_key, shape, spread, most, split=(), held_as=jnp.bfloat16):
    result = jax.random.normal(own_key, shape, jnp.float32) * spread
    if len(split) > 0:
        result = shard_levels(own_key, shape, split, -0.22, 0.18) * result
    return jnp.clip(result, min=-most, max=most).astype(held_as)


def setup_inputs(seed: int = 0, part: int = 0) -> dict:
    key_of = jax.random.split(jax.random.key(seed), 8)
    part_keys = jax.random.split(jax.random.fold_in(key_of[7], part), 8)
    hidden = noise(part_keys[0], (N_DP, N_EXPERT, ROUTED_EXPERTS, CAP, HIDDEN_HALF), 1.0, 6.0, ((0, 2), (2, 8)))
    expert_choice_index_keys = jax.random.split(jax.random.fold_in(part_keys[1], 1), TOKENS // TOK_DEV)
    expert_choice_index_turns = jax.random.permutation(jax.random.fold_in(part_keys[1], 3), TOKENS // TOK_DEV)
    expert_choice_index = jax.vmap(lambda own, number: deal_out(jax.random.fold_in(part_keys[1], 2), own, number, TOK_DEV, ROUTED_EXPERTS, TOP, CAP, 2))(expert_choice_index_keys, expert_choice_index_turns).reshape((TOKENS, TOP))
    gates = jnp.clip(0.02 + 0.28 * jax.random.uniform(part_keys[2], (TOKENS, TOP), jnp.float32) ** shard_levels(part_keys[2], (TOKENS, TOP), ((0, 16),), -0.2, 0.2), 0.02, 0.3)
    down_adapter_hidden = noise(key_of[3], (ROUTED_EXPERTS, ADAPTER_RANK, HIDDEN_HALF), HIDDEN_HALF ** -0.5, 0.15625, ((0, 8), (2, 2)))
    hidden_tangent = noise(part_keys[4], (ROUTED_EXPERTS, ADAPTER_RANK, HIDDEN_HALF), HIDDEN_HALF ** -0.5, 0.15625, ((0, 8), (2, 2)))
    down_adapter_output = noise(key_of[5], (ROUTED_EXPERTS, ADAPTER_RANK, MODEL_WIDTH), ADAPTER_RANK ** -0.5, 1.0, ((0, 8),))
    output_tangent_factor = noise(part_keys[6], (ROUTED_EXPERTS, ADAPTER_RANK, MODEL_WIDTH), ADAPTER_RANK ** -0.5, 1.0, ((0, 8),))
    return {"hidden": hidden, "expert_choice_index": expert_choice_index, "gates": gates, "down_adapter_hidden": down_adapter_hidden, "hidden_tangent": hidden_tangent, "down_adapter_output": down_adapter_output, "output_tangent_factor": output_tangent_factor}


def slot_positions(expert_choice_index):
    blocks = expert_choice_index.reshape(-1, TOK_DEV * TOP)
    labels = jnp.arange(ROUTED_EXPERTS, dtype=jnp.int32)
    matches = (blocks[:, :, None] == labels[None, None, :]).astype(jnp.int32)
    before = jnp.cumsum(matches, axis=1) - matches
    slot_index = jnp.sum(before * matches, axis=2)
    position = blocks * CAP + slot_index
    return position.astype(jnp.int32).reshape(N_DP, N_EXPERT, TOK_DEV, TOP)


def reference(hidden, expert_choice_index, gates, down_adapter_hidden, hidden_tangent, down_adapter_output, output_tangent_factor):
    positions = slot_positions(expert_choice_index)
    gate_blocks = gates.reshape(N_DP, N_EXPERT, TOK_DEV, TOP)
    adapter_set = jnp.concatenate([down_adapter_hidden, hidden_tangent], axis=1).astype(jnp.float32)
    left_output_factor = down_adapter_output.astype(jnp.float32)
    right_b = output_tangent_factor.astype(jnp.float32)

    def pick_rows(rows, place):
        return rows[place]

    def place_rows(place, rows):
        empty = jnp.zeros((ROUTED_EXPERTS * CAP, MODEL_WIDTH), jnp.bfloat16)
        return empty.at[place.reshape(-1)].set(rows.reshape(-1, MODEL_WIDTH))

    def group_terms(carry, inputs):
        cached, place, gate_rows = inputs
        cached_wide = cached.astype(jnp.float32)
        projected_result = jnp.einsum("secf,erf->secr", cached_wide, adapter_set).astype(jnp.bfloat16)
        projected_hidden = projected_result[..., :ADAPTER_RANK]
        projected_model = projected_result[..., ADAPTER_RANK:]
        tangent_row_block = jnp.einsum("pibx,ixm->pibm", projected_model.astype(jnp.float32), left_output_factor)
        tangent_row_block = tangent_row_block + jnp.einsum("pibx,ixm->pibm", projected_hidden.astype(jnp.float32), right_b)
        tangent_row_block = tangent_row_block.astype(jnp.bfloat16).reshape(N_EXPERT, ROUTED_EXPERTS * CAP, MODEL_WIDTH)
        picked = jax.vmap(pick_rows)(tangent_row_block, place).astype(jnp.float32)
        output_tangent = jnp.sum(gate_rows[..., None] * picked, axis=2)
        cot_rows = (gate_rows[..., None] * output_tangent[:, :, None, :]).astype(jnp.bfloat16)
        cot_buffer = jax.vmap(place_rows)(place, cot_rows).reshape(N_EXPERT, ROUTED_EXPERTS, CAP, MODEL_WIDTH)
        cot_wide = cot_buffer.astype(jnp.float32)
        back_proj = jnp.einsum("pzot,zat->pzoa", cot_wide, left_output_factor).astype(jnp.bfloat16)
        part_a = jnp.einsum("secr,secf->erf", back_proj.astype(jnp.float32), cached_wide)
        part_b = jnp.einsum("secr,secd->erd", projected_hidden.astype(jnp.float32), cot_wide)
        return (carry[0] + part_a, carry[1] + part_b), None

    start = (jnp.zeros((ROUTED_EXPERTS, ADAPTER_RANK, HIDDEN_HALF), jnp.float32), jnp.zeros((ROUTED_EXPERTS, ADAPTER_RANK, MODEL_WIDTH), jnp.float32))
    totals, unused = lax.scan(group_terms, start, (hidden, positions, gate_blocks))
    return totals[0], totals[1]
```

```python
import jax
import jax.numpy as jnp
from jax import lax
from jax.sharding import PartitionSpec as P

F32 = jnp.float32
BF16 = jnp.bfloat16


def split_two(x):
    high = x.astype(BF16)
    low = (x - high.astype(F32)).astype(BF16)
    return high, low


def routing_tables(expert_choice_index, gates, experts):
    labels = jnp.arange(experts, dtype=jnp.int32)
    matches = expert_choice_index[:, :, None] == labels[None, None, :]
    weight = jnp.sum(jnp.where(matches, gates[:, :, None], 0.0), axis=1)
    chosen = jnp.any(matches, axis=1)
    tokens = expert_choice_index.shape[0]
    earlier = jnp.tril(jnp.ones((tokens, tokens), BF16), -1)
    before = jnp.dot(earlier, chosen.astype(BF16), preferred_element_type=F32)
    position = jnp.where(chosen, before, -1.0)
    return position, weight


def on_device(
    hidden,
    expert_choice_index,
    gates,
    down_adapter_hidden,
    hidden_tangent,
    down_adapter_output,
    output_tangent_factor,
):
    cached = hidden[0]
    groups, exp_dev, slots_per, hidden_width = cached.shape
    rank = down_adapter_output.shape[1]
    layer_width = down_adapter_output.shape[2]
    shards = lax.axis_size("dp")
    experts = groups * exp_dev
    share_a = hidden_width // shards
    share_b = layer_width // shards
    me = lax.axis_index("expert")
    dp = lax.axis_index("dp")

    adapter_pieces = jnp.concatenate([down_adapter_hidden, hidden_tangent], axis=1)
    adapter_set = lax.all_gather(adapter_pieces, "dp", axis=2, tiled=True)
    stacked = jnp.concatenate([output_tangent_factor, down_adapter_output], axis=1)
    stacked_share = lax.dynamic_slice_in_dim(stacked, dp * share_b, share_b, 2)
    factors = lax.all_gather(stacked_share, "expert", axis=0, tiled=True)
    factors = factors.reshape(experts * 2 * rank, share_b)

    position, weight = routing_tables(expert_choice_index, gates, experts)
    tables = lax.all_gather(jnp.concatenate([position, weight], axis=1), "expert", axis=0)
    position, weight = tables[:, :, :experts], tables[:, :, experts:]

    projected = jnp.einsum("secf,erf->secr", cached, adapter_set, preferred_element_type=F32)
    projected = lax.all_gather(projected.astype(BF16), "expert", axis=1, tiled=True)
    places = jnp.arange(slots_per, dtype=jnp.int32).astype(F32)
    onehot = (position[:, :, :, None] == places).astype(BF16)
    rows = jnp.einsum("stxc,sxcr->stxr", onehot, projected, preferred_element_type=F32)
    rows = weight[:, :, :, None] * rows
    tokens = rows.shape[0] * rows.shape[1]
    mine = lax.dynamic_slice_in_dim(rows, me * exp_dev, exp_dev, 2)[..., :rank]
    mine = mine.reshape(tokens, exp_dev * rank)
    rows = rows.reshape(tokens, experts * 2 * rank)
    rows_b = rows.astype(BF16)

    mixing = jnp.einsum("na,nb->ab", mine.astype(BF16), rows_b, preferred_element_type=F32)
    own_output = lax.dynamic_slice_in_dim(down_adapter_output, dp * share_b, share_b, 2)
    gram = jnp.einsum(
        "rm,eam->rea", factors, own_output, preferred_element_type=F32
    ).reshape(experts * 2 * rank, exp_dev * rank)
    gram, mixing = lax.psum((gram, mixing), "dp")

    high, low = split_two(mixing)
    grad_b = jnp.dot(high, factors, preferred_element_type=F32)
    grad_b = grad_b + jnp.dot(low, factors, preferred_element_type=F32)
    grad_b = grad_b.reshape(exp_dev, rank, share_b)

    back = jnp.dot(rows_b, gram.astype(BF16), preferred_element_type=F32)
    back = back.reshape(groups, -1, exp_dev, rank)
    own_weight = lax.dynamic_slice_in_dim(weight, me * exp_dev, exp_dev, 2)
    back = (back * own_weight[..., None]).astype(BF16)
    own_onehot = lax.dynamic_slice_in_dim(onehot, me * exp_dev, exp_dev, 2)
    back_slots = jnp.einsum(
        "stec,ster->secr", own_onehot, back, preferred_element_type=F32
    ).astype(BF16)
    part_a = jnp.einsum("secr,secf->erf", back_slots, cached, preferred_element_type=F32)
    grad_a = lax.psum_scatter(part_a, "dp", scatter_dimension=2, tiled=True)
    return (grad_a, grad_b)


def solution(mesh):
    placed = (
        P(("dom", "dp"), None, "expert", None, None),
        P(("dom", "dp", "expert"), None),
        P(("dom", "dp", "expert"), None),
        P("expert", None, "dp"),
        P(("dom", "expert"), None, "dp"),
        P("expert", None, None),
        P(("dom", "expert"), None, None),
    )
    return jax.shard_map(
        on_device,
        mesh=mesh,
        in_specs=placed,
        out_specs=(P(("dom", "expert"), None, "dp"), P(("dom", "expert"), None, "dp")),
        check_vma=False,
    )
```

```python
import functools

import jax
import jax.numpy as jnp
from jax import lax
from jax.experimental import pallas as pl
from jax.experimental.pallas import tpu as pltpu
from jax.sharding import PartitionSpec as P

F32 = jnp.float32
BF16 = jnp.bfloat16
MESH = pl.DeviceIdType.MESH


def split_two(x):
    high = x.astype(BF16)
    low = (x - high.astype(F32)).astype(BF16)
    return high, low


def routing_tables(expert_choice_index, gates, experts):
    labels = jnp.arange(experts, dtype=jnp.int32)
    matches = expert_choice_index[:, :, None] == labels[None, None, :]
    weight = jnp.sum(jnp.where(matches, gates[:, :, None], 0.0), axis=1)
    chosen = jnp.any(matches, axis=1)
    tokens = expert_choice_index.shape[0]
    earlier = jnp.tril(jnp.ones((tokens, tokens), BF16), -1)
    before = jnp.dot(earlier, chosen.astype(BF16), preferred_element_type=F32)
    position = jnp.where(chosen, before, -1.0)
    return position, weight


def on_device_collectives(
    hidden,
    expert_choice_index,
    gates,
    down_adapter_hidden,
    hidden_tangent,
    down_adapter_output,
    output_tangent_factor,
):
    cached = hidden[0]
    groups, exp_dev, slots_per, hidden_width = cached.shape
    rank = down_adapter_output.shape[1]
    layer_width = down_adapter_output.shape[2]
    shards = lax.axis_size("dp")
    experts = groups * exp_dev
    share_a = hidden_width // shards
    share_b = layer_width // shards
    me = lax.axis_index("expert")
    dp = lax.axis_index("dp")

    adapter_pieces = jnp.concatenate([down_adapter_hidden, hidden_tangent], axis=1)
    adapter_set = lax.all_gather(adapter_pieces, "dp", axis=2, tiled=True)
    stacked = jnp.concatenate([output_tangent_factor, down_adapter_output], axis=1)
    stacked_share = lax.dynamic_slice_in_dim(stacked, dp * share_b, share_b, 2)
    factors = lax.all_gather(stacked_share, "expert", axis=0, tiled=True)
    factors = factors.reshape(experts * 2 * rank, share_b)

    position, weight = routing_tables(expert_choice_index, gates, experts)
    tables = lax.all_gather(jnp.concatenate([position, weight], axis=1), "expert", axis=0)
    position, weight = tables[:, :, :experts], tables[:, :, experts:]

    projected = jnp.einsum("secf,erf->secr", cached, adapter_set, preferred_element_type=F32)
    projected = lax.all_gather(projected.astype(BF16), "expert", axis=1, tiled=True)
    places = jnp.arange(slots_per, dtype=jnp.int32).astype(F32)
    onehot = (position[:, :, :, None] == places).astype(BF16)
    rows = jnp.einsum("stxc,sxcr->stxr", onehot, projected, preferred_element_type=F32)
    rows = weight[:, :, :, None] * rows
    tokens = rows.shape[0] * rows.shape[1]
    mine = lax.dynamic_slice_in_dim(rows, me * exp_dev, exp_dev, 2)[..., :rank]
    mine = mine.reshape(tokens, exp_dev * rank)
    rows = rows.reshape(tokens, experts * 2 * rank)
    rows_b = rows.astype(BF16)

    mixing = jnp.einsum("na,nb->ab", mine.astype(BF16), rows_b, preferred_element_type=F32)
    own_output = lax.dynamic_slice_in_dim(down_adapter_output, dp * share_b, share_b, 2)
    gram = jnp.einsum(
        "rm,eam->rea", factors, own_output, preferred_element_type=F32
    ).reshape(experts * 2 * rank, exp_dev * rank)
    gram, mixing = lax.psum((gram, mixing), "dp")

    high, low = split_two(mixing)
    grad_b = jnp.dot(high, factors, preferred_element_type=F32)
    grad_b = grad_b + jnp.dot(low, factors, preferred_element_type=F32)
    grad_b = grad_b.reshape(exp_dev, rank, share_b)

    back = jnp.dot(rows_b, gram.astype(BF16), preferred_element_type=F32)
    back = back.reshape(groups, -1, exp_dev, rank)
    own_weight = lax.dynamic_slice_in_dim(weight, me * exp_dev, exp_dev, 2)
    back = (back * own_weight[..., None]).astype(BF16)
    own_onehot = lax.dynamic_slice_in_dim(onehot, me * exp_dev, exp_dev, 2)
    back_slots = jnp.einsum(
        "stec,ster->secr", own_onehot, back, preferred_element_type=F32
    ).astype(BF16)
    part_a = jnp.einsum("secr,secf->erf", back_slots, cached, preferred_element_type=F32)
    grad_a = lax.psum_scatter(part_a, "dp", scatter_dimension=2, tiled=True)
    return (grad_a, grad_b)


NT = (((1,), (1,)), ((), ()))
TN = (((0,), (0,)), ((), ()))


def dot(a, b, dims=(((1,), (0,)), ((), ()))):
    return lax.dot_general(a, b, dims, preferred_element_type=F32)


def fused_kernel(
    n, rank, slots,
    hidden, own_factors, own_adapters, own_table,
    grad_a, grad_b,
    factors, adapters, tables, proj_wide, proj, rows_of,
    g_high, g_low, mix, mix_core, mix_sum, mix_dp, gram, gram_core, gram_sum, gram_dp,
    back, pa, pa_in, gb, gb_in,
    f_send, f_recv, p_send, p_recv, t_send, t_recv, m_send, m_recv, local,
):
    me = lax.axis_index("expert")
    x = lax.axis_index("dp")
    core = lax.rem(me, 2)
    chip = me // 2
    blocks = hidden.shape[0]
    half = blocks // 2
    padded = proj.shape[1]
    experts = 2 * n
    wide = factors.shape[2]
    share = 2 * wide
    depth = own_adapters.shape[1]
    tokens = tables.shape[2]
    two = 2 * rank
    pair = 2 * two
    quad = 4 * rank

    barrier = pltpu.get_barrier_semaphore()
    for d in range(1, n):
        pl.semaphore_signal(
            barrier, inc=1, device_id={"expert": lax.rem(me + d, n)}, device_id_type=MESH
        )
    pl.semaphore_signal(barrier, inc=1, device_id={"dp": 1 - x}, device_id_type=MESH)
    pl.semaphore_wait(barrier, n)

    def to_dp(k, src, dst):
        return pltpu.make_async_remote_copy(
            src_ref=src, dst_ref=dst, send_sem=m_send.at[k], recv_sem=m_recv.at[k],
            device_id={"dp": 1 - x}, device_id_type=MESH,
        )

    def to_core(k, src, dst):
        return pltpu.make_async_remote_copy(
            src_ref=src, dst_ref=dst, send_sem=m_send.at[k], recv_sem=m_recv.at[k],
            device_id={"expert": me + 1 - 2 * core}, device_id_type=MESH,
        )

    def to_peer(d, src, dst, send, recv):
        return pltpu.make_async_remote_copy(
            src_ref=src, dst_ref=dst, send_sem=send.at[d], recv_sem=recv.at[d],
            device_id={"expert": lax.rem(me + d, n)}, device_id_type=MESH,
        )

    def columns_of(c):
        return pl.ds(pl.multiple_of(x * share + c * wide, 128), wide)

    adapter_copy = to_dp(0, own_adapters, adapters)
    adapter_copy.start()
    t_copies, f_copies, p_copies = {}, {}, {}
    for d in range(1, n):
        t_copies[d] = to_peer(d, own_table, tables.at[me], t_send, t_recv)
        t_copies[d].start()
        c_to = lax.rem(me + d, 2)
        f_copies[d] = to_peer(d, own_factors.at[:, columns_of(c_to)], factors.at[me], f_send, f_recv)
        p_copies[d] = to_peer(d, proj.at[pl.ds(half * c_to, half)], rows_of.at[me], p_send, p_recv)
    order = [d for k in range(1, n // 2 + 1) for d in sorted({k, n - k})]
    early = order[: max(1, n // 2 - 1)]
    late = [d for d in order if d not in early]
    for d in early:
        f_copies[d].start()
    f_local = pltpu.make_async_copy(own_factors.at[:, columns_of(core)], factors.at[me], local.at[0])
    f_local.start()
    t_local = pltpu.make_async_copy(own_table, tables.at[me], local.at[1])
    t_local.start()

    proj_wide[...] = jnp.zeros_like(proj_wide)
    own_cols = pl.ds(pl.multiple_of(x * depth, 128), depth)
    far_cols = pl.ds(pl.multiple_of((1 - x) * depth, 128), depth)
    for s in range(blocks):
        parts = [
            dot(hidden[s, j, :, own_cols], own_adapters[j * two:(j + 1) * two, :], NT)
            for j in range(2)
        ]
        proj_wide[s, 0:slots, :] = jnp.concatenate(parts, axis=1)
    adapter_copy.wait_recv()
    for s in range(blocks):
        parts = [
            dot(hidden[s, j, :, far_cols], adapters[j * two:(j + 1) * two, :], NT)
            for j in range(2)
        ]
        proj_wide[s, 0:slots, :] = proj_wide[s, 0:slots, :] + jnp.concatenate(parts, axis=1)
        proj[s] = proj_wide[s].astype(BF16)
    for d in order:
        p_copies[d].start()
    for d in late:
        f_copies[d].start()
    p_local = pltpu.make_async_copy(proj.at[pl.ds(half * core, half)], rows_of.at[me], local.at[2])
    p_local.start()

    places = lax.broadcasted_iota(jnp.int32, (padded, tokens), 0).astype(F32)

    def onehot(position):
        return jnp.where(places == position, 1.0, 0.0).astype(BF16)

    t_local.wait()
    for d in range(1, n):
        t_copies[d].wait_recv()
    p_local.wait()
    for d in range(0, n):
        if d:
            p_copies[d].wait_recv()
        q = lax.rem(me + n - d, n)
        for t in range(half):
            block = half * core + t
            marks = jnp.concatenate(
                [onehot(tables[block, pl.ds(2 * q + j, 1), :]) for j in range(2)], axis=1
            )
            both = dot(rows_of[q, t], marks, TN)
            for j in range(2):
                weight = tables[block, pl.ds(experts + 2 * q + j, 1), :]
                piece = both[j * two:(j + 1) * two, j * tokens:(j + 1) * tokens] * weight
                high = piece.astype(BF16)
                where = pl.ds(pl.multiple_of(q * pair + j * two, two), two)
                g_high[where, t * tokens:(t + 1) * tokens] = high
                g_low[where, t * tokens:(t + 1) * tokens] = (piece - high.astype(F32)).astype(BF16)

    def chip_rows(ref, offset):
        return jnp.concatenate(
            [
                ref[pl.ds(pl.multiple_of(chip * 4 * two + i * two + offset, rank), rank), :]
                for i in range(4)
            ],
            axis=0,
        )

    a_high = chip_rows(g_high, 0)
    a_low = chip_rows(g_low, 0)
    a_both = jnp.concatenate([a_high, a_low], axis=0)
    tile = 2 * pair
    for r in range(0, experts * two, tile):
        first = dot(a_both, g_high[r:r + tile, :], NT)
        second = dot(a_high, g_low[r:r + tile, :], NT)
        mix[:, r:r + tile] = first[:quad] + first[quad:] + second
    mix_copy = to_core(1, mix, mix_core)
    mix_copy.start()
    mix_copy.wait_recv()
    mix_sum[...] = mix[...] + mix_core[...]
    mix_dp_copy = to_dp(2, mix_sum, mix_dp)
    mix_dp_copy.start()

    f_local.wait()
    sibling = me + 1 - 2 * core
    waited = set()
    f_copies[1].wait_recv()
    f_copies[n - 1].wait_recv()
    waited = {0, 1, n - 1}
    outs = jnp.concatenate(
        [
            factors[2 * chip + i, j * two + rank:(j + 1) * two, :]
            for i in range(2)
            for j in range(2)
        ],
        axis=0,
    )
    for d in [0] + order:
        if d not in waited:
            f_copies[d].wait_recv()
        q = lax.rem(me + n - d, n)
        gram[:, pl.ds(pl.multiple_of(q * pair, pair), pair)] = dot(outs, factors[q], NT)
    gram_copy = to_core(3, gram, gram_core)
    gram_copy.start()
    gram_copy.wait_recv()
    gram_sum[...] = gram[...] + gram_core[...]
    gram_dp_copy = to_dp(4, gram_sum, gram_dp)
    gram_dp_copy.start()

    mix_dp_copy.wait_recv()
    m_high, m_low = split_two(mix_sum[...] + mix_dp[...])
    m_both = jnp.concatenate([m_high, m_low], axis=0)
    total = None
    for q in range(n):
        term = dot(m_both[:, q * pair:(q + 1) * pair], factors[q])
        total = term if total is None else total + term
    gb[...] = total[:quad] + total[quad:]
    gb_copy = to_core(5, gb.at[pl.ds(pl.multiple_of((1 - core) * two, two), two)], gb_in)
    gb_copy.start()
    mine = pl.ds(pl.multiple_of(core * wide, 128), wide)
    other = pl.ds(pl.multiple_of((1 - core) * wide, 128), wide)
    grad_b[:, mine] = gb[pl.ds(pl.multiple_of(core * two, two), two), :]

    gram_dp_copy.wait_recv()
    k_high, k_low = split_two(gram_sum[...] + gram_dp[...])
    k_both = jnp.concatenate([k_high, k_low], axis=0)
    for t in range(half):
        cols = slice(t * tokens, (t + 1) * tokens)
        first = dot(k_both, g_high[:, cols])
        value = first[:quad] + first[quad:] + dot(k_high, g_low[:, cols])
        block = half * core + t
        for i in range(4):
            weight = tables[block, pl.ds(experts + 4 * chip + i, 1), :]
            piece = value[i * rank:(i + 1) * rank] * weight
            back[core, i * rank:(i + 1) * rank, cols] = piece.astype(BF16)
    back_copy = to_core(
        6,
        back.at[core, pl.ds(pl.multiple_of((1 - core) * two, two), two)],
        back.at[core, pl.ds(pl.multiple_of((1 - core) * two, two), two)],
    )
    back_copy.start()
    back_copy.wait_recv()
    for j in range(2):
        acc = None
        for s in range(blocks):
            t = s % half
            rows = back[
                s // half,
                pl.ds(pl.multiple_of(core * two + j * rank, rank), rank),
                t * tokens:(t + 1) * tokens,
            ]
            placed = dot(rows, onehot(tables[s, pl.ds(2 * me + j, 1), :]), NT).astype(BF16)
            term = dot(placed[:, :slots], hidden[s, j])
            acc = term if acc is None else acc + term
        for h in range(2):
            pa[h, j * rank:(j + 1) * rank, :] = acc[:, h * depth:(h + 1) * depth]
    pa_copy = to_dp(7, pa.at[1 - x], pa_in)
    pa_copy.start()
    gb_copy.wait_recv()
    grad_b[:, other] = gb_in[...]
    pa_copy.wait_recv()
    grad_a[...] = pa[x] + pa_in[...]

    for d in range(1, n):
        t_copies[d].wait_send()
        f_copies[d].wait_send()
        p_copies[d].wait_send()
    for copy in (
        adapter_copy, mix_copy, mix_dp_copy, gram_copy, gram_dp_copy, gb_copy, back_copy, pa_copy
    ):
        copy.wait_send()


def on_device(
    hidden,
    expert_choice_index,
    gates,
    down_adapter_hidden,
    hidden_tangent,
    down_adapter_output,
    output_tangent_factor,
):
    n = lax.axis_size("expert")
    exp_dev, rank, depth = down_adapter_hidden.shape
    layer_width = down_adapter_output.shape[2]
    blocks, _, slots, hidden_width = hidden.shape[1:]
    tokens = expert_choice_index.shape[0]
    fits = (
        lax.axis_size("dp") == 2 and n % 2 == 0 and exp_dev == 2 and rank == 32
        and tokens == 128 and depth % 128 == 0 and layer_width % 512 == 0
    )
    if not fits:
        return on_device_collectives(
            hidden, expert_choice_index, gates, down_adapter_hidden, hidden_tangent,
            down_adapter_output, output_tangent_factor,
        )
    experts = exp_dev * n
    wide = layer_width // 4
    padded = -(-slots // 16) * 16
    half = blocks // 2
    all_rows = experts * 2 * rank
    own_adapters = jnp.concatenate([down_adapter_hidden, hidden_tangent], axis=1)
    own_factors = jnp.concatenate([output_tangent_factor, down_adapter_output], axis=1)
    position, weight = routing_tables(expert_choice_index, gates, experts)
    own_table = jnp.concatenate([position, weight], axis=1).T
    dma = pltpu.SemaphoreType.DMA
    square = pltpu.VMEM((4 * rank, all_rows), F32)
    grad_a, grad_b = pl.pallas_call(
        functools.partial(fused_kernel, n, rank, slots),
        out_shape=(
            jax.ShapeDtypeStruct((2 * rank, depth), F32),
            jax.ShapeDtypeStruct((2 * rank, 2 * wide), F32),
        ),
        in_specs=[pl.BlockSpec(memory_space=pltpu.VMEM)] * 4,
        out_specs=[pl.BlockSpec(memory_space=pltpu.VMEM)] * 2,
        scratch_shapes=[
            pltpu.VMEM((n, 4 * rank, wide), BF16),
            pltpu.VMEM((4 * rank, depth), BF16),
            pltpu.VMEM((n, 2 * experts, tokens), F32),
            pltpu.VMEM((blocks, padded, 4 * rank), F32),
            pltpu.VMEM((blocks, padded, 4 * rank), BF16),
            pltpu.VMEM((n, half, padded, 4 * rank), BF16),
            pltpu.VMEM((all_rows, half * tokens), BF16),
            pltpu.VMEM((all_rows, half * tokens), BF16),
        ] + [square] * 8 + [
            pltpu.VMEM((2, 4 * rank, half * tokens), BF16),
            pltpu.VMEM((2, 2 * rank, depth), F32),
            pltpu.VMEM((2 * rank, depth), F32),
            pltpu.VMEM((4 * rank, wide), F32),
            pltpu.VMEM((2 * rank, wide), F32),
            dma((n,)), dma((n,)), dma((n,)), dma((n,)), dma((n,)), dma((n,)),
            dma((8,)), dma((8,)), dma((3,)),
        ],
        compiler_params=pltpu.CompilerParams(
            collective_id=0, has_side_effects=True, vmem_limit_bytes=48 * 1024 * 1024
        ),
    )(
        hidden[0],
        own_factors.reshape(4 * rank, layer_width),
        own_adapters.reshape(4 * rank, depth),
        own_table,
    )
    return grad_a.reshape(2, rank, depth), grad_b.reshape(2, rank, 2 * wide)


def solution(mesh):
    placed = (
        P(("dom", "dp"), None, "expert", None, None),
        P(("dom", "dp", "expert"), None),
        P(("dom", "dp", "expert"), None),
        P("expert", None, "dp"),
        P(("dom", "expert"), None, "dp"),
        P("expert", None, None),
        P(("dom", "expert"), None, None),
    )
    return jax.shard_map(
        on_device,
        mesh=mesh,
        in_specs=placed,
        out_specs=(P(("dom", "expert"), None, "dp"), P(("dom", "expert"), None, "dp")),
        check_vma=False,
    )
```

```python
import functools

import jax
import jax.numpy as jnp
from jax import lax
from jax.experimental import pallas as pl
from jax.experimental.pallas import tpu as pltpu
from jax.sharding import PartitionSpec as P

F32 = jnp.float32
BF16 = jnp.bfloat16
MESH = pl.DeviceIdType.MESH


def split_two(x):
    high = x.astype(BF16)
    low = (x - high.astype(F32)).astype(BF16)
    return high, low


def routing_tables(expert_choice_index, gates, experts):
    labels = jnp.arange(experts, dtype=jnp.int32)
    matches = expert_choice_index[:, :, None] == labels[None, None, :]
    weight = jnp.sum(jnp.where(matches, gates[:, :, None], 0.0), axis=1)
    chosen = jnp.any(matches, axis=1)
    tokens = expert_choice_index.shape[0]
    earlier = jnp.tril(jnp.ones((tokens, tokens), BF16), -1)
    before = jnp.dot(earlier, chosen.astype(BF16), preferred_element_type=F32)
    position = jnp.where(chosen, before, -1.0)
    return position, weight


def on_device_collectives(
    hidden,
    expert_choice_index,
    gates,
    down_adapter_hidden,
    hidden_tangent,
    down_adapter_output,
    output_tangent_factor,
):
    cached = hidden[0]
    groups, exp_dev, slots_per, hidden_width = cached.shape
    rank = down_adapter_output.shape[1]
    layer_width = down_adapter_output.shape[2]
    shards = lax.axis_size("dp")
    experts = groups * exp_dev
    share_a = hidden_width // shards
    share_b = layer_width // shards
    me = lax.axis_index("expert")
    dp = lax.axis_index("dp")

    adapter_pieces = jnp.concatenate([down_adapter_hidden, hidden_tangent], axis=1)
    adapter_set = lax.all_gather(adapter_pieces, "dp", axis=2, tiled=True)
    stacked = jnp.concatenate([output_tangent_factor, down_adapter_output], axis=1)
    stacked_share = lax.dynamic_slice_in_dim(stacked, dp * share_b, share_b, 2)
    factors = lax.all_gather(stacked_share, "expert", axis=0, tiled=True)
    factors = factors.reshape(experts * 2 * rank, share_b)

    position, weight = routing_tables(expert_choice_index, gates, experts)
    tables = lax.all_gather(jnp.concatenate([position, weight], axis=1), "expert", axis=0)
    position, weight = tables[:, :, :experts], tables[:, :, experts:]

    projected = jnp.einsum("secf,erf->secr", cached, adapter_set, preferred_element_type=F32)
    projected = lax.all_gather(projected.astype(BF16), "expert", axis=1, tiled=True)
    places = jnp.arange(slots_per, dtype=jnp.int32).astype(F32)
    onehot = (position[:, :, :, None] == places).astype(BF16)
    rows = jnp.einsum("stxc,sxcr->stxr", onehot, projected, preferred_element_type=F32)
    rows = weight[:, :, :, None] * rows
    tokens = rows.shape[0] * rows.shape[1]
    mine = lax.dynamic_slice_in_dim(rows, me * exp_dev, exp_dev, 2)[..., :rank]
    mine = mine.reshape(tokens, exp_dev * rank)
    rows = rows.reshape(tokens, experts * 2 * rank)
    rows_b = rows.astype(BF16)

    mixing = jnp.einsum("na,nb->ab", mine.astype(BF16), rows_b, preferred_element_type=F32)
    own_output = lax.dynamic_slice_in_dim(down_adapter_output, dp * share_b, share_b, 2)
    gram = jnp.einsum(
        "rm,eam->rea", factors, own_output, preferred_element_type=F32
    ).reshape(experts * 2 * rank, exp_dev * rank)
    gram, mixing = lax.psum((gram, mixing), "dp")

    high, low = split_two(mixing)
    grad_b = jnp.dot(high, factors, preferred_element_type=F32)
    grad_b = grad_b + jnp.dot(low, factors, preferred_element_type=F32)
    grad_b = grad_b.reshape(exp_dev, rank, share_b)

    back = jnp.dot(rows_b, gram.astype(BF16), preferred_element_type=F32)
    back = back.reshape(groups, -1, exp_dev, rank)
    own_weight = lax.dynamic_slice_in_dim(weight, me * exp_dev, exp_dev, 2)
    back = (back * own_weight[..., None]).astype(BF16)
    own_onehot = lax.dynamic_slice_in_dim(onehot, me * exp_dev, exp_dev, 2)
    back_slots = jnp.einsum(
        "stec,ster->secr", own_onehot, back, preferred_element_type=F32
    ).astype(BF16)
    part_a = jnp.einsum("secr,secf->erf", back_slots, cached, preferred_element_type=F32)
    grad_a = lax.psum_scatter(part_a, "dp", scatter_dimension=2, tiled=True)
    return (grad_a, grad_b)


NT = (((1,), (1,)), ((), ()))
TN = (((0,), (0,)), ((), ()))


def dot(a, b, dims=(((1,), (0,)), ((), ()))):
    return lax.dot_general(a, b, dims, preferred_element_type=F32)


def fused_kernel(
    n, rank, slots,
    hidden, own_factors, own_adapters, own_table,
    grad_a, grad_b,
    factors, adapters, tables, proj_wide, proj, rows_of,
    g_high, g_low, mix, mix_core, mix_sum, gram, gram_core, gram_sum, mix_out, mix_dp, gram_out, gram_dp,
    back, pa, pa_in, gb, gb_in,
    f_send, f_recv, p_send, p_recv, t_send, t_recv, h_send, h_recv, m_send, m_recv, local,
):
    me = lax.axis_index("expert")
    x = lax.axis_index("dp")
    y = lax.axis_index("dom")
    core = lax.rem(me, 2)
    chip = me // 2
    blocks = hidden.shape[0]
    half = blocks // 2
    padded = proj.shape[1]
    experts = 2 * n
    wide = factors.shape[2]
    share = 2 * wide
    depth = own_adapters.shape[1]
    tokens = tables.shape[2]
    two = 2 * rank
    pair = 2 * two
    quad = 4 * rank

    barrier = pltpu.get_barrier_semaphore()
    for d in range(1, n):
        pl.semaphore_signal(
            barrier, inc=1, device_id={"expert": lax.rem(me + d, n)}, device_id_type=MESH
        )
    pl.semaphore_signal(barrier, inc=1, device_id={"dp": 1 - x}, device_id_type=MESH)
    pl.semaphore_signal(barrier, inc=1, device_id={"dom": 1 - y}, device_id_type=MESH)
    pl.semaphore_wait(barrier, n + 1)

    def to_dp(k, src, dst):
        return pltpu.make_async_remote_copy(
            src_ref=src, dst_ref=dst, send_sem=m_send.at[k], recv_sem=m_recv.at[k],
            device_id={"dp": 1 - x}, device_id_type=MESH,
        )

    def to_core(k, src, dst):
        return pltpu.make_async_remote_copy(
            src_ref=src, dst_ref=dst, send_sem=m_send.at[k], recv_sem=m_recv.at[k],
            device_id={"expert": me + 1 - 2 * core}, device_id_type=MESH,
        )

    def to_peer(d, src, dst, send, recv):
        return pltpu.make_async_remote_copy(
            src_ref=src, dst_ref=dst, send_sem=send.at[d], recv_sem=recv.at[d],
            device_id={"expert": lax.rem(me + d, n)}, device_id_type=MESH,
        )

    def columns_of(c):
        return pl.ds(pl.multiple_of(x * share + c * wide, 128), wide)

    adapter_copy = to_dp(0, own_adapters, adapters)
    adapter_copy.start()
    t_copies, f_copies, p_copies, h_copies = {}, {}, {}, {}
    for d in range(1, n):
        t_copies[d] = to_peer(d, own_table, tables.at[me], t_send, t_recv)
        t_copies[d].start()
        c_to = lax.rem(me + d, 2)
        kept = pl.ds(pl.multiple_of(y * rank, rank), 3 * rank)
        f_copies[d] = to_peer(
            d, own_factors.at[kept, columns_of(c_to)], factors.at[me, kept], f_send, f_recv
        )
        given = pl.ds(pl.multiple_of(y * 3 * rank, rank), rank)
        source = lax.rem(me + n - d, n)
        h_copies[d] = pltpu.make_async_remote_copy(
            src_ref=factors.at[source, given], dst_ref=factors.at[source, given],
            send_sem=h_send.at[d], recv_sem=h_recv.at[d],
            device_id={"dom": 1 - y}, device_id_type=MESH,
        )
        p_copies[d] = to_peer(d, proj.at[pl.ds(half * c_to, half)], rows_of.at[me], p_send, p_recv)
    order = [d for k in range(1, n // 2 + 1) for d in sorted({k, n - k})]
    early = order[: max(1, n // 2 - 1)]
    late = [d for d in order if d not in early]
    for d in early:
        f_copies[d].start()
    f_local = pltpu.make_async_copy(own_factors.at[:, columns_of(core)], factors.at[me], local.at[0])
    f_local.start()
    t_local = pltpu.make_async_copy(own_table, tables.at[me], local.at[1])
    t_local.start()

    proj_wide[...] = jnp.zeros_like(proj_wide)
    own_cols = pl.ds(pl.multiple_of(x * depth, 128), depth)
    far_cols = pl.ds(pl.multiple_of((1 - x) * depth, 128), depth)
    for s in range(blocks):
        parts = [
            dot(hidden[s, j, :, own_cols], own_adapters[j * two:(j + 1) * two, :], NT)
            for j in range(2)
        ]
        proj_wide[s, 0:slots, :] = jnp.concatenate(parts, axis=1)
    adapter_copy.wait_recv()
    for s in range(blocks):
        parts = [
            dot(hidden[s, j, :, far_cols], adapters[j * two:(j + 1) * two, :], NT)
            for j in range(2)
        ]
        proj_wide[s, 0:slots, :] = proj_wide[s, 0:slots, :] + jnp.concatenate(parts, axis=1)
        proj[s] = proj_wide[s].astype(BF16)
    for d in order:
        p_copies[d].start()
    for d in late:
        f_copies[d].start()
    p_local = pltpu.make_async_copy(proj.at[pl.ds(half * core, half)], rows_of.at[me], local.at[2])
    p_local.start()

    places = lax.broadcasted_iota(jnp.int32, (padded, tokens), 0).astype(F32)

    def onehot(position):
        return jnp.where(places == position, 1.0, 0.0).astype(BF16)

    t_local.wait()
    for d in range(1, n):
        t_copies[d].wait_recv()
    p_local.wait()
    for d in range(0, n):
        if d:
            p_copies[d].wait_recv()
        q = lax.rem(me + n - d, n)
        for t in range(half):
            block = half * core + t
            marks = jnp.concatenate(
                [onehot(tables[block, pl.ds(2 * q + j, 1), :]) for j in range(2)], axis=1
            )
            both = dot(rows_of[q, t], marks, TN)
            for j in range(2):
                weight = tables[block, pl.ds(experts + 2 * q + j, 1), :]
                piece = both[j * two:(j + 1) * two, j * tokens:(j + 1) * tokens] * weight
                high = piece.astype(BF16)
                where = pl.ds(pl.multiple_of(q * pair + j * two, two), two)
                g_high[where, t * tokens:(t + 1) * tokens] = high
                g_low[where, t * tokens:(t + 1) * tokens] = (piece - high.astype(F32)).astype(BF16)

    def chip_rows(ref):
        return jnp.concatenate(
            [
                ref[pl.ds(pl.multiple_of(chip * 4 * two + first, rank), rank), :]
                for first in (rank, two, pair + rank, pair + two)
            ],
            axis=0,
        )

    core_rows = pl.ds(pl.multiple_of(core * two, two), two)

    def hand_over(d):
        f_copies[d].wait_recv()
        h_copies[d].start()

    for d in early:
        hand_over(d)
    a_high = chip_rows(g_high)
    a_low = chip_rows(g_low)
    a_both = jnp.concatenate([a_high, a_low], axis=0)
    tile = 2 * pair
    for r in range(0, experts * two, tile):
        first = dot(a_both, g_high[r:r + tile, :], NT)
        second = dot(a_high, g_low[r:r + tile, :], NT)
        mix[:, r:r + tile] = first[:quad] + first[quad:] + second
    mix_copy = to_core(1, mix, mix_core)
    mix_copy.start()
    mix_copy.wait_recv()
    mix_sum[...] = mix[...] + mix_core[...]
    mix_out[...] = mix_sum[core_rows, :].astype(BF16)
    mix_dp_copy = to_dp(2, mix_out, mix_dp.at[core])
    mix_dp_copy.start()
    for d in late:
        hand_over(d)
    mix_dp_copy.wait_recv()
    mix_share = to_core(8, mix_dp.at[core], mix_dp.at[core])
    mix_share.start()

    def both_cores(ref):
        return jnp.concatenate([ref[0], ref[1]], axis=0).astype(F32)

    f_local.wait()
    h_copies[1].wait_recv()
    h_copies[n - 1].wait_recv()
    waited = {0, 1, n - 1}
    outs = jnp.concatenate(
        [
            factors[2 * chip + i, first:first + rank, :]
            for i in range(2)
            for first in (0, 3 * rank)
        ],
        axis=0,
    )
    for d in [0] + order:
        if d not in waited:
            h_copies[d].wait_recv()
        q = lax.rem(me + n - d, n)
        gram[:, pl.ds(pl.multiple_of(q * pair, pair), pair)] = dot(outs, factors[q], NT)
    gram_copy = to_core(3, gram, gram_core)
    gram_copy.start()
    gram_copy.wait_recv()
    gram_sum[...] = gram[...] + gram_core[...]
    gram_out[...] = gram_sum[core_rows, :].astype(BF16)
    gram_dp_copy = to_dp(4, gram_out, gram_dp.at[core])
    gram_dp_copy.start()

    mix_share.wait_recv()
    m_high, m_low = split_two(mix_sum[...] + both_cores(mix_dp))
    m_both = jnp.concatenate([m_high, m_low], axis=0)
    total = None
    for q in range(n):
        if q == n // 2:
            gram_dp_copy.wait_recv()
            gram_share = to_core(9, gram_dp.at[core], gram_dp.at[core])
            gram_share.start()
        term = dot(m_both[:, q * pair:(q + 1) * pair], factors[q])
        total = term if total is None else total + term
    gb[...] = total[:quad] + total[quad:]
    gb_copy = to_core(5, gb.at[pl.ds(pl.multiple_of((1 - core) * two, two), two)], gb_in)
    gb_copy.start()
    mine = pl.ds(pl.multiple_of(core * wide, 128), wide)
    other = pl.ds(pl.multiple_of((1 - core) * wide, 128), wide)
    grad_b[:, mine] = gb[pl.ds(pl.multiple_of(core * two, two), two), :]

    gram_share.wait_recv()
    k_high, k_low = split_two(gram_sum[...] + both_cores(gram_dp))
    k_both = jnp.concatenate([k_high, k_low], axis=0)
    for t in range(half):
        cols = slice(t * tokens, (t + 1) * tokens)
        first = dot(k_both, g_high[:, cols])
        value = first[:quad] + first[quad:] + dot(k_high, g_low[:, cols])
        block = half * core + t
        for i in range(4):
            weight = tables[block, pl.ds(experts + 4 * chip + i, 1), :]
            piece = value[i * rank:(i + 1) * rank] * weight
            back[core, i * rank:(i + 1) * rank, cols] = piece.astype(BF16)
    back_copy = to_core(
        6,
        back.at[core, pl.ds(pl.multiple_of((1 - core) * two, two), two)],
        back.at[core, pl.ds(pl.multiple_of((1 - core) * two, two), two)],
    )
    back_copy.start()
    back_copy.wait_recv()
    for j in range(2):
        acc = None
        for s in range(blocks):
            t = s % half
            rows = back[
                s // half,
                pl.ds(pl.multiple_of(core * two + j * rank, rank), rank),
                t * tokens:(t + 1) * tokens,
            ]
            placed = dot(rows, onehot(tables[s, pl.ds(2 * me + j, 1), :]), NT).astype(BF16)
            term = dot(placed[:, :slots], hidden[s, j])
            acc = term if acc is None else acc + term
        for h in range(2):
            pa[h, j * rank:(j + 1) * rank, :] = acc[:, h * depth:(h + 1) * depth]
    pa_copy = to_dp(7, pa.at[1 - x], pa_in)
    pa_copy.start()
    gb_copy.wait_recv()
    grad_b[:, other] = gb_in[...]
    pa_copy.wait_recv()
    grad_a[...] = pa[x] + pa_in[...]

    for d in range(1, n):
        t_copies[d].wait_send()
        f_copies[d].wait_send()
        p_copies[d].wait_send()
        h_copies[d].wait_send()
    for copy in (
        mix_share, gram_share,
        adapter_copy, mix_copy, mix_dp_copy, gram_copy, gram_dp_copy, gb_copy, back_copy, pa_copy
    ):
        copy.wait_send()


def on_device(
    hidden,
    expert_choice_index,
    gates,
    down_adapter_hidden,
    hidden_tangent,
    down_adapter_output,
    output_tangent_factor,
):
    n = lax.axis_size("expert")
    exp_dev, rank, depth = down_adapter_hidden.shape
    layer_width = down_adapter_output.shape[2]
    blocks, _, slots, hidden_width = hidden.shape[1:]
    tokens = expert_choice_index.shape[0]
    fits = (
        lax.axis_size("dp") == 2 and lax.axis_size("dom") == 2 and n % 2 == 0 and exp_dev == 2 and rank == 32
        and tokens == 128 and depth % 128 == 0 and layer_width % 512 == 0
    )
    if not fits:
        return on_device_collectives(
            hidden, expert_choice_index, gates, down_adapter_hidden, hidden_tangent,
            down_adapter_output, output_tangent_factor,
        )
    experts = exp_dev * n
    wide = layer_width // 4
    padded = -(-slots // 16) * 16
    half = blocks // 2
    all_rows = experts * 2 * rank
    own_adapters = jnp.concatenate(
        [hidden_tangent[0], down_adapter_hidden[0], down_adapter_hidden[1], hidden_tangent[1]]
    )
    own_factors = jnp.concatenate(
        [
            down_adapter_output[0], output_tangent_factor[0],
            output_tangent_factor[1], down_adapter_output[1],
        ]
    )
    position, weight = routing_tables(expert_choice_index, gates, experts)
    own_table = jnp.concatenate([position, weight], axis=1).T
    dma = pltpu.SemaphoreType.DMA
    narrow = pltpu.VMEM((2 * rank, all_rows), BF16)
    paired = pltpu.VMEM((2, 2 * rank, all_rows), BF16)
    square = pltpu.VMEM((4 * rank, all_rows), F32)
    grad_a, grad_b = pl.pallas_call(
        functools.partial(fused_kernel, n, rank, slots),
        out_shape=(
            jax.ShapeDtypeStruct((2 * rank, depth), F32),
            jax.ShapeDtypeStruct((2 * rank, 2 * wide), F32),
        ),
        in_specs=[pl.BlockSpec(memory_space=pltpu.VMEM)] * 4,
        out_specs=[pl.BlockSpec(memory_space=pltpu.VMEM)] * 2,
        scratch_shapes=[
            pltpu.VMEM((n, 4 * rank, wide), BF16),
            pltpu.VMEM((4 * rank, depth), BF16),
            pltpu.VMEM((n, 2 * experts, tokens), F32),
            pltpu.VMEM((blocks, padded, 4 * rank), F32),
            pltpu.VMEM((blocks, padded, 4 * rank), BF16),
            pltpu.VMEM((n, half, padded, 4 * rank), BF16),
            pltpu.VMEM((all_rows, half * tokens), BF16),
            pltpu.VMEM((all_rows, half * tokens), BF16),
        ] + [square] * 6 + [narrow, paired, narrow, paired] + [
            pltpu.VMEM((2, 4 * rank, half * tokens), BF16),
            pltpu.VMEM((2, 2 * rank, depth), F32),
            pltpu.VMEM((2 * rank, depth), F32),
            pltpu.VMEM((4 * rank, wide), F32),
            pltpu.VMEM((2 * rank, wide), F32),
            dma((n,)), dma((n,)), dma((n,)), dma((n,)), dma((n,)), dma((n,)), dma((n,)), dma((n,)),
            dma((10,)), dma((10,)), dma((3,)),
        ],
        compiler_params=pltpu.CompilerParams(
            collective_id=0, has_side_effects=True, vmem_limit_bytes=48 * 1024 * 1024
        ),
    )(
        hidden[0],
        own_factors,
        own_adapters,
        own_table,
    )
    return grad_a.reshape(2, rank, depth), grad_b.reshape(2, rank, 2 * wide)


def solution(mesh):
    placed = (
        P(("dom", "dp"), None, "expert", None, None),
        P(("dom", "dp", "expert"), None),
        P(("dom", "dp", "expert"), None),
        P("expert", None, "dp"),
        P(("dom", "expert"), None, "dp"),
        P("expert", None, None),
        P(("dom", "expert"), None, None),
    )
    return jax.shard_map(
        on_device,
        mesh=mesh,
        in_specs=placed,
        out_specs=(P(("dom", "expert"), None, "dp"), P(("dom", "expert"), None, "dp")),
        check_vma=False,
    )
```

```python
import functools

import jax
import jax.numpy as jnp
from jax import lax
from jax.experimental import pallas as pl
from jax.experimental.pallas import tpu as pltpu
from jax.sharding import PartitionSpec as P

F32 = jnp.float32
BF16 = jnp.bfloat16
MESH = pl.DeviceIdType.MESH


def split_two(x):
    high = x.astype(BF16)
    low = (x - high.astype(F32)).astype(BF16)
    return high, low


def routing_tables(expert_choice_index, gates, experts):
    labels = jnp.arange(experts, dtype=jnp.int32)
    matches = expert_choice_index[:, :, None] == labels[None, None, :]
    weight = jnp.sum(jnp.where(matches, gates[:, :, None], 0.0), axis=1)
    chosen = jnp.any(matches, axis=1)
    tokens = expert_choice_index.shape[0]
    earlier = jnp.tril(jnp.ones((tokens, tokens), BF16), -1)
    before = jnp.dot(earlier, chosen.astype(BF16), preferred_element_type=F32)
    position = jnp.where(chosen, before, -1.0)
    return position, weight


def on_device_collectives(
    hidden,
    expert_choice_index,
    gates,
    down_adapter_hidden,
    hidden_tangent,
    down_adapter_output,
    output_tangent_factor,
):
    cached = hidden[0]
    groups, exp_dev, slots_per, hidden_width = cached.shape
    rank = down_adapter_output.shape[1]
    layer_width = down_adapter_output.shape[2]
    shards = lax.axis_size("dp")
    experts = groups * exp_dev
    share_a = hidden_width // shards
    share_b = layer_width // shards
    me = lax.axis_index("expert")
    dp = lax.axis_index("dp")

    adapter_pieces = jnp.concatenate([down_adapter_hidden, hidden_tangent], axis=1)
    adapter_set = lax.all_gather(adapter_pieces, "dp", axis=2, tiled=True)
    stacked = jnp.concatenate([output_tangent_factor, down_adapter_output], axis=1)
    stacked_share = lax.dynamic_slice_in_dim(stacked, dp * share_b, share_b, 2)
    factors = lax.all_gather(stacked_share, "expert", axis=0, tiled=True)
    factors = factors.reshape(experts * 2 * rank, share_b)

    position, weight = routing_tables(expert_choice_index, gates, experts)
    tables = lax.all_gather(jnp.concatenate([position, weight], axis=1), "expert", axis=0)
    position, weight = tables[:, :, :experts], tables[:, :, experts:]

    projected = jnp.einsum("secf,erf->secr", cached, adapter_set, preferred_element_type=F32)
    projected = lax.all_gather(projected.astype(BF16), "expert", axis=1, tiled=True)
    places = jnp.arange(slots_per, dtype=jnp.int32).astype(F32)
    onehot = (position[:, :, :, None] == places).astype(BF16)
    rows = jnp.einsum("stxc,sxcr->stxr", onehot, projected, preferred_element_type=F32)
    rows = weight[:, :, :, None] * rows
    tokens = rows.shape[0] * rows.shape[1]
    mine = lax.dynamic_slice_in_dim(rows, me * exp_dev, exp_dev, 2)[..., :rank]
    mine = mine.reshape(tokens, exp_dev * rank)
    rows = rows.reshape(tokens, experts * 2 * rank)
    rows_b = rows.astype(BF16)

    mixing = jnp.einsum("na,nb->ab", mine.astype(BF16), rows_b, preferred_element_type=F32)
    own_output = lax.dynamic_slice_in_dim(down_adapter_output, dp * share_b, share_b, 2)
    gram = jnp.einsum(
        "rm,eam->rea", factors, own_output, preferred_element_type=F32
    ).reshape(experts * 2 * rank, exp_dev * rank)
    gram, mixing = lax.psum((gram, mixing), "dp")

    high, low = split_two(mixing)
    grad_b = jnp.dot(high, factors, preferred_element_type=F32)
    grad_b = grad_b + jnp.dot(low, factors, preferred_element_type=F32)
    grad_b = grad_b.reshape(exp_dev, rank, share_b)

    back = jnp.dot(rows_b, gram.astype(BF16), preferred_element_type=F32)
    back = back.reshape(groups, -1, exp_dev, rank)
    own_weight = lax.dynamic_slice_in_dim(weight, me * exp_dev, exp_dev, 2)
    back = (back * own_weight[..., None]).astype(BF16)
    own_onehot = lax.dynamic_slice_in_dim(onehot, me * exp_dev, exp_dev, 2)
    back_slots = jnp.einsum(
        "stec,ster->secr", own_onehot, back, preferred_element_type=F32
    ).astype(BF16)
    part_a = jnp.einsum("secr,secf->erf", back_slots, cached, preferred_element_type=F32)
    grad_a = lax.psum_scatter(part_a, "dp", scatter_dimension=2, tiled=True)
    return (grad_a, grad_b)


NT = (((1,), (1,)), ((), ()))
TN = (((0,), (0,)), ((), ()))


def dot(a, b, dims=(((1,), (0,)), ((), ()))):
    return lax.dot_general(a, b, dims, preferred_element_type=F32)


def fused_kernel(
    n, rank, slots,
    hidden, own_factors, own_adapters, own_table,
    grad_a, grad_b,
    factors, adapters, tables, proj_wide, proj, rows_of,
    g_high, g_low, mix, mix_core, mix_sum, gram, gram_core, gram_sum, mix_out, mix_dp, gram_out, gram_dp,
    back, pa, pa_out, pa_in, gb, gb_in,
    f_send, f_recv, p_send, p_recv, t_send, t_recv, h_send, h_recv, m_send, m_recv, local,
):
    me = lax.axis_index("expert")
    x = lax.axis_index("dp")
    y = lax.axis_index("dom")
    core = lax.rem(me, 2)
    chip = me // 2
    blocks = hidden.shape[0]
    half = blocks // 2
    padded = proj.shape[1]
    experts = 2 * n
    wide = factors.shape[2]
    share = 2 * wide
    depth = own_adapters.shape[1]
    tokens = tables.shape[2]
    two = 2 * rank
    pair = 2 * two
    quad = 4 * rank

    barrier = pltpu.get_barrier_semaphore()
    for d in range(1, n):
        pl.semaphore_signal(
            barrier, inc=1, device_id={"expert": lax.rem(me + d, n)}, device_id_type=MESH
        )
    pl.semaphore_signal(barrier, inc=1, device_id={"dp": 1 - x}, device_id_type=MESH)
    pl.semaphore_signal(barrier, inc=1, device_id={"dom": 1 - y}, device_id_type=MESH)
    pl.semaphore_wait(barrier, n + 1)

    def to_dp(k, src, dst):
        return pltpu.make_async_remote_copy(
            src_ref=src, dst_ref=dst, send_sem=m_send.at[k], recv_sem=m_recv.at[k],
            device_id={"dp": 1 - x}, device_id_type=MESH,
        )

    def to_core(k, src, dst):
        return pltpu.make_async_remote_copy(
            src_ref=src, dst_ref=dst, send_sem=m_send.at[k], recv_sem=m_recv.at[k],
            device_id={"expert": me + 1 - 2 * core}, device_id_type=MESH,
        )

    def to_peer(d, src, dst, send, recv):
        return pltpu.make_async_remote_copy(
            src_ref=src, dst_ref=dst, send_sem=send.at[d], recv_sem=recv.at[d],
            device_id={"expert": lax.rem(me + d, n)}, device_id_type=MESH,
        )

    def columns_of(c):
        return pl.ds(pl.multiple_of(x * share + c * wide, 128), wide)

    adapter_copy = to_dp(0, own_adapters, adapters)
    adapter_copy.start()
    t_copies, f_copies, p_copies, h_copies = {}, {}, {}, {}
    for d in range(1, n):
        t_copies[d] = to_peer(d, own_table, tables.at[me], t_send, t_recv)
        t_copies[d].start()
        c_to = lax.rem(me + d, 2)
        kept = pl.ds(pl.multiple_of(y * rank, rank), 3 * rank)
        f_copies[d] = to_peer(
            d, own_factors.at[kept, columns_of(c_to)], factors.at[me, kept], f_send, f_recv
        )
        given = pl.ds(pl.multiple_of(y * 3 * rank, rank), rank)
        source = lax.rem(me + n - d, n)
        h_copies[d] = pltpu.make_async_remote_copy(
            src_ref=factors.at[source, given], dst_ref=factors.at[source, given],
            send_sem=h_send.at[d], recv_sem=h_recv.at[d],
            device_id={"dom": 1 - y}, device_id_type=MESH,
        )
        p_copies[d] = to_peer(d, proj.at[pl.ds(half * c_to, half)], rows_of.at[me], p_send, p_recv)
    order = [d for k in range(1, n // 2 + 1) for d in sorted({k, n - k})]
    early = order[: max(1, n // 2 - 1)]
    late = [d for d in order if d not in early]
    for d in early:
        f_copies[d].start()
    f_local = pltpu.make_async_copy(own_factors.at[:, columns_of(core)], factors.at[me], local.at[0])
    f_local.start()
    t_local = pltpu.make_async_copy(own_table, tables.at[me], local.at[1])
    t_local.start()

    proj_wide[...] = jnp.zeros_like(proj_wide)
    own_cols = pl.ds(pl.multiple_of(x * depth, 128), depth)
    far_cols = pl.ds(pl.multiple_of((1 - x) * depth, 128), depth)
    for s in range(blocks):
        parts = [
            dot(hidden[s, j, :, own_cols], own_adapters[j * two:(j + 1) * two, :], NT)
            for j in range(2)
        ]
        proj_wide[s, 0:slots, :] = jnp.concatenate(parts, axis=1)
    adapter_copy.wait_recv()
    for s in range(blocks):
        parts = [
            dot(hidden[s, j, :, far_cols], adapters[j * two:(j + 1) * two, :], NT)
            for j in range(2)
        ]
        proj_wide[s, 0:slots, :] = proj_wide[s, 0:slots, :] + jnp.concatenate(parts, axis=1)
        proj[s] = proj_wide[s].astype(BF16)
    for d in order:
        p_copies[d].start()
    for d in late:
        f_copies[d].start()
    p_local = pltpu.make_async_copy(proj.at[pl.ds(half * core, half)], rows_of.at[me], local.at[2])
    p_local.start()

    places = lax.broadcasted_iota(jnp.int32, (padded, tokens), 0).astype(F32)

    def onehot(position):
        return jnp.where(places == position, 1.0, 0.0).astype(BF16)

    t_local.wait()
    for d in range(1, n):
        t_copies[d].wait_recv()
    p_local.wait()
    for d in range(0, n):
        if d:
            p_copies[d].wait_recv()
        q = lax.rem(me + n - d, n)
        for t in range(half):
            block = half * core + t
            marks = jnp.concatenate(
                [onehot(tables[block, pl.ds(2 * q + j, 1), :]) for j in range(2)], axis=1
            )
            both = dot(rows_of[q, t], marks, TN)
            for j in range(2):
                weight = tables[block, pl.ds(experts + 2 * q + j, 1), :]
                piece = both[j * two:(j + 1) * two, j * tokens:(j + 1) * tokens] * weight
                high = piece.astype(BF16)
                where = pl.ds(pl.multiple_of(q * pair + j * two, two), two)
                g_high[where, t * tokens:(t + 1) * tokens] = high
                g_low[where, t * tokens:(t + 1) * tokens] = (piece - high.astype(F32)).astype(BF16)

    def chip_rows(ref):
        return jnp.concatenate(
            [
                ref[pl.ds(pl.multiple_of(chip * 4 * two + first, rank), rank), :]
                for first in (rank, two, pair + rank, pair + two)
            ],
            axis=0,
        )

    core_rows = pl.ds(pl.multiple_of(core * two, two), two)

    def hand_over(d):
        f_copies[d].wait_recv()
        h_copies[d].start()

    for d in early:
        hand_over(d)
    a_high = chip_rows(g_high)
    a_low = chip_rows(g_low)
    a_both = jnp.concatenate([a_high, a_low], axis=0)
    tile = 2 * pair
    for r in range(0, experts * two, tile):
        first = dot(a_both, g_high[r:r + tile, :], NT)
        second = dot(a_high, g_low[r:r + tile, :], NT)
        mix[:, r:r + tile] = first[:quad] + first[quad:] + second
    mix_copy = to_core(1, mix, mix_core)
    mix_copy.start()
    mix_copy.wait_recv()
    mix_sum[...] = mix[...] + mix_core[...]
    mix_out[...] = mix_sum[core_rows, :].astype(BF16)
    mix_dp_copy = to_dp(2, mix_out, mix_dp.at[core])
    mix_dp_copy.start()
    for d in late:
        hand_over(d)
    mix_dp_copy.wait_recv()
    mix_share = to_core(8, mix_dp.at[core], mix_dp.at[core])
    mix_share.start()

    def both_cores(ref):
        return jnp.concatenate([ref[0], ref[1]], axis=0).astype(F32)

    f_local.wait()
    h_copies[1].wait_recv()
    h_copies[n - 1].wait_recv()
    waited = {0, 1, n - 1}
    outs = jnp.concatenate(
        [
            factors[2 * chip + i, first:first + rank, :]
            for i in range(2)
            for first in (0, 3 * rank)
        ],
        axis=0,
    )
    for d in [0] + order:
        if d not in waited:
            h_copies[d].wait_recv()
        q = lax.rem(me + n - d, n)
        gram[:, pl.ds(pl.multiple_of(q * pair, pair), pair)] = dot(outs, factors[q], NT)
    gram_copy = to_core(3, gram, gram_core)
    gram_copy.start()
    gram_copy.wait_recv()
    gram_sum[...] = gram[...] + gram_core[...]
    gram_out[...] = gram_sum[core_rows, :].astype(BF16)
    gram_dp_copy = to_dp(4, gram_out, gram_dp.at[core])
    gram_dp_copy.start()

    mix_share.wait_recv()
    m_high, m_low = split_two(mix_sum[...] + both_cores(mix_dp))
    m_both = jnp.concatenate([m_high, m_low], axis=0)
    total = None
    for q in range(n):
        if q == n // 2:
            gram_dp_copy.wait_recv()
            gram_share = to_core(9, gram_dp.at[core], gram_dp.at[core])
            gram_share.start()
        term = dot(m_both[:, q * pair:(q + 1) * pair], factors[q])
        total = term if total is None else total + term
    gb[...] = total[:quad] + total[quad:]
    gb_copy = to_core(5, gb.at[pl.ds(pl.multiple_of((1 - core) * two, two), two)], gb_in)
    gb_copy.start()
    mine = pl.ds(pl.multiple_of(core * wide, 128), wide)
    other = pl.ds(pl.multiple_of((1 - core) * wide, 128), wide)
    grad_b[:, mine] = gb[pl.ds(pl.multiple_of(core * two, two), two), :]

    gram_share.wait_recv()
    k_high, k_low = split_two(gram_sum[...] + both_cores(gram_dp))
    k_both = jnp.concatenate([k_high, k_low], axis=0)
    for t in range(half):
        cols = slice(t * tokens, (t + 1) * tokens)
        first = dot(k_both, g_high[:, cols])
        value = first[:quad] + first[quad:] + dot(k_high, g_low[:, cols])
        block = half * core + t
        for i in range(4):
            weight = tables[block, pl.ds(experts + 4 * chip + i, 1), :]
            piece = value[i * rank:(i + 1) * rank] * weight
            back[core, i * rank:(i + 1) * rank, cols] = piece.astype(BF16)
    back_copy = to_core(
        6,
        back.at[core, pl.ds(pl.multiple_of((1 - core) * two, two), two)],
        back.at[core, pl.ds(pl.multiple_of((1 - core) * two, two), two)],
    )
    back_copy.start()
    back_copy.wait_recv()
    for j in range(2):
        acc = None
        for s in range(blocks):
            t = s % half
            rows = back[
                s // half,
                pl.ds(pl.multiple_of(core * two + j * rank, rank), rank),
                t * tokens:(t + 1) * tokens,
            ]
            placed = dot(rows, onehot(tables[s, pl.ds(2 * me + j, 1), :]), NT).astype(BF16)
            term = dot(placed[:, :slots], hidden[s, j])
            acc = term if acc is None else acc + term
        for h in range(2):
            pa[h, j * rank:(j + 1) * rank, :] = acc[:, h * depth:(h + 1) * depth]
    pa_out[...] = pa[1 - x].astype(BF16)
    pa_copy = to_dp(7, pa_out, pa_in)
    pa_copy.start()
    gb_copy.wait_recv()
    grad_b[:, other] = gb_in[...]
    pa_copy.wait_recv()
    grad_a[...] = pa[x] + pa_in[...].astype(F32)

    for d in range(1, n):
        t_copies[d].wait_send()
        f_copies[d].wait_send()
        p_copies[d].wait_send()
        h_copies[d].wait_send()
    for copy in (
        mix_share, gram_share,
        adapter_copy, mix_copy, mix_dp_copy, gram_copy, gram_dp_copy, gb_copy, back_copy, pa_copy
    ):
        copy.wait_send()


def on_device(
    hidden,
    expert_choice_index,
    gates,
    down_adapter_hidden,
    hidden_tangent,
    down_adapter_output,
    output_tangent_factor,
):
    n = lax.axis_size("expert")
    exp_dev, rank, depth = down_adapter_hidden.shape
    layer_width = down_adapter_output.shape[2]
    blocks, _, slots, hidden_width = hidden.shape[1:]
    tokens = expert_choice_index.shape[0]
    fits = (
        lax.axis_size("dp") == 2 and lax.axis_size("dom") == 2 and n % 2 == 0 and exp_dev == 2 and rank == 32
        and tokens == 128 and depth % 128 == 0 and layer_width % 512 == 0
    )
    if not fits:
        return on_device_collectives(
            hidden, expert_choice_index, gates, down_adapter_hidden, hidden_tangent,
            down_adapter_output, output_tangent_factor,
        )
    experts = exp_dev * n
    wide = layer_width // 4
    padded = -(-slots // 16) * 16
    half = blocks // 2
    all_rows = experts * 2 * rank
    own_adapters = jnp.concatenate(
        [hidden_tangent[0], down_adapter_hidden[0], down_adapter_hidden[1], hidden_tangent[1]]
    )
    own_factors = jnp.concatenate(
        [
            down_adapter_output[0], output_tangent_factor[0],
            output_tangent_factor[1], down_adapter_output[1],
        ]
    )
    position, weight = routing_tables(expert_choice_index, gates, experts)
    own_table = jnp.concatenate([position, weight], axis=1).T
    dma = pltpu.SemaphoreType.DMA
    narrow = pltpu.VMEM((2 * rank, all_rows), BF16)
    paired = pltpu.VMEM((2, 2 * rank, all_rows), BF16)
    square = pltpu.VMEM((4 * rank, all_rows), F32)
    grad_a, grad_b = pl.pallas_call(
        functools.partial(fused_kernel, n, rank, slots),
        out_shape=(
            jax.ShapeDtypeStruct((2 * rank, depth), F32),
            jax.ShapeDtypeStruct((2 * rank, 2 * wide), F32),
        ),
        in_specs=[pl.BlockSpec(memory_space=pltpu.VMEM)] * 4,
        out_specs=[pl.BlockSpec(memory_space=pltpu.VMEM)] * 2,
        scratch_shapes=[
            pltpu.VMEM((n, 4 * rank, wide), BF16),
            pltpu.VMEM((4 * rank, depth), BF16),
            pltpu.VMEM((n, 2 * experts, tokens), F32),
            pltpu.VMEM((blocks, padded, 4 * rank), F32),
            pltpu.VMEM((blocks, padded, 4 * rank), BF16),
            pltpu.VMEM((n, half, padded, 4 * rank), BF16),
            pltpu.VMEM((all_rows, half * tokens), BF16),
            pltpu.VMEM((all_rows, half * tokens), BF16),
        ] + [square] * 6 + [narrow, paired, narrow, paired] + [
            pltpu.VMEM((2, 4 * rank, half * tokens), BF16),
            pltpu.VMEM((2, 2 * rank, depth), F32),
            pltpu.VMEM((2 * rank, depth), BF16),
            pltpu.VMEM((2 * rank, depth), BF16),
            pltpu.VMEM((4 * rank, wide), F32),
            pltpu.VMEM((2 * rank, wide), F32),
            dma((n,)), dma((n,)), dma((n,)), dma((n,)), dma((n,)), dma((n,)), dma((n,)), dma((n,)),
            dma((10,)), dma((10,)), dma((3,)),
        ],
        compiler_params=pltpu.CompilerParams(
            collective_id=0, has_side_effects=True, vmem_limit_bytes=48 * 1024 * 1024
        ),
    )(
        hidden[0],
        own_factors,
        own_adapters,
        own_table,
    )
    return grad_a.reshape(2, rank, depth), grad_b.reshape(2, rank, 2 * wide)


def solution(mesh):
    placed = (
        P(("dom", "dp"), None, "expert", None, None),
        P(("dom", "dp", "expert"), None),
        P(("dom", "dp", "expert"), None),
        P("expert", None, "dp"),
        P(("dom", "expert"), None, "dp"),
        P("expert", None, None),
        P(("dom", "expert"), None, None),
    )
    return jax.shard_map(
        on_device,
        mesh=mesh,
        in_specs=placed,
        out_specs=(P(("dom", "expert"), None, "dp"), P(("dom", "expert"), None, "dp")),
        check_vma=False,
    )
```
